32 devices in a mesh: dev: 32 (over z, y, x, core).
Axes of the slice: x: 2, y: 2, z: 4, core: 2. Of those that a mesh axis runs over, the one named last changes fastest.
Arguments:
- queries: bfloat16 [64, 32, 128], P('dev'), may hold values from -0.119628906 to 0.119628906
- passages: bfloat16 [16384, 64, 128], P('dev'), may hold values from -1.796875 to 1.796875
- lengths: int32 [16384], P('dev'), may hold values from 16 to 64
- candidates: int32 [64, 64], P('dev'), may hold values from 0 to 16383, as said below
Outputs:
- scores: float32 [64, 64], P('dev')
The draws below stay inside these ranges and needn't reach their ends.
Inputs may be any that keep to these rules, and one draw needn't show every extreme that they name: `candidates`: the 128 entries of the rows held by one device name, with repetition, at most 8 passages held by any one device (passage p is held by device p // 512), and exactly 8 for four devices; the passages of low number within each device are named far more often than the others, and a few devices are named far more often than the others over all rows.
All inputs are finite; a program needn't handle non-finite values.
Results may differ from the reference program's by a relative error of at most 0.0003.
Values may be sent and summed in bfloat16 or wider, within the bound.
No kernel may reach another device: no remote copies, remote signals or barrier semaphores. Data moves between devices by JAX's collectives and lax.ppermute only.
A program may use at most 64 MiB of HBM per device.

```python
import jax
import jax.numpy as jnp
from jax import lax

DIM = 128
QTOK = 32
PTOK = 64
CAND = 64
Q_DEV = 2
P_DEV = 512
QUERIES = 64
NPASS = 16384
CAP = 8
N_DEV = 32


def draw_candidates(key, part):
    slots = Q_DEV * CAND
    count = N_DEV
    pool = jax.random.permutation(jax.random.fold_in(key, 1), count)[:8]

    def one_device(dkey):
        k_hot, k_rank, k_order, k_local = jax.random.split(dkey, 4)
        hot = pool[jax.random.permutation(k_hot, 8)[:4]]
        frequent_flag = jnp.zeros((count,), jnp.int32).at[hot].set(1)
        ranks = jax.random.permutation(k_rank, count).astype(jnp.int32)
        order = jnp.argsort(frequent_flag * count + ranks, stable=True)
        cold = order[:count - 4]
        index = jnp.arange(slots)
        hot_part = index < 4 * CAP
        owner = jnp.where(hot_part, hot[jnp.minimum(index // CAP, 3)], cold[(index - 4 * CAP) % (count - 4)])
        owner = owner[jax.random.permutation(k_order, slots)]
        draws = jax.random.randint(k_local, (slots,), 0, 1024)
        local = draws * draws // 1024 * draws // 1024 * P_DEV // 1024
        return (owner * P_DEV + local).astype(jnp.int32)
    keys = jax.random.split(jax.random.fold_in(key, 2), count)
    return jax.vmap(one_device)(keys).reshape(QUERIES, CAND)


def with_ends(values, key, smallest, largest):
    index_at = [jax.random.randint(jax.random.fold_in(key, axis), (), 0, length) for axis, length in enumerate(values.shape)]
    main_axis = values.shape.index(max(values.shape))
    beside = index_at[:main_axis] + [(index_at[main_axis] + 1) % values.shape[main_axis]] + index_at[main_axis + 1:]
    return values.at[tuple(index_at)].set(smallest).at[tuple(beside)].set(largest)


def level_of(rng, extent, shards, smallest, top_value):
    factor_of = 1.0
    for axis_at, shards_of in shards:
        steps = jax.random.uniform(jax.random.fold_in(jax.random.fold_in(rng, 6), axis_at), (shards_of,), jnp.float32, smallest / len(shards), top_value / len(shards))
        factor_of = factor_of * jnp.repeat(jnp.exp(steps), extent[axis_at] // shards_of).reshape((-1,) + (1,) * (len(extent) - 1 - axis_at))
    return factor_of


def scatter_about(rng, extent, spread, bound, pieces=(), kind=jnp.bfloat16):
    loudness = level_of(rng, extent, pieces, -0.22, 0.18) if pieces else 1.0
    array = jax.random.normal(rng, extent, jnp.float32) * spread * loudness
    return jnp.minimum(jnp.maximum(array, -bound), bound).astype(kind)


def setup_inputs(seed: int = 0) -> dict:
    splits = jax.random.split(jax.random.key(seed), 5)
    return {
        "queries": scatter_about(splits[0], (QUERIES, QTOK, DIM), 0.02, 0.119628906, ((0, 32),)),
        "passages": scatter_about(splits[1], (NPASS, PTOK, DIM), 0.3, 1.796875, ((0, 32),)),
        "lengths": with_ends(jax.random.randint(splits[2], (NPASS,), max(1, PTOK // 4), PTOK + 1), jax.random.fold_in(splits[2], 1), max(1, PTOK // 4), PTOK).astype(jnp.int32),
        "candidates": draw_candidates(jax.random.fold_in(splits[4], 71), 0),
    }


def reference(queries, passages, lengths, candidates):
    def one_query(item):
        query, ids = item
        block_groups = passages[ids].astype(jnp.float32)
        live = lengths[ids]
        similarity_matrix = jnp.einsum("qd,ctd->cqt", query.astype(jnp.float32), block_groups)
        keep = jnp.arange(PTOK)[None, None, :] < live[:, None, None]
        masked = jnp.where(keep, similarity_matrix, -1e30)
        return jnp.sum(jnp.max(masked, axis=2), axis=1)

    return lax.map(one_query, (queries, candidates))
```

```python
import functools

import jax
import jax.numpy as jnp
from jax import lax
from jax.experimental import pallas as pl
from jax.experimental.pallas import tpu as pltpu
from jax.sharding import PartitionSpec as P

MESH_BITS = 2
SHORTEST = 16
NT = (((1,), (1,)), ((), ()))
ID_ROWS = 8


def stages_of(count):
    stages, high = [], count.bit_length() - 1
    while high > 0:
        width = min(MESH_BITS, high)
        stages.append((high - width, 1 << width))
        high -= width
    return stages


def order_of(stage):
    return (1, 3, 2) if stage == 0 else (1, 2, 3)


def flips_of(stages):
    flips = [0]
    for stage, (shift, size) in enumerate(stages):
        flips = [flip ^ ((digit << shift) | 1 if digit else 0) for digit in (0,) + order_of(stage) for flip in flips]
    return flips


def gather_blocks(block, stages, count):
    line = marked = None
    for stage, (shift, size) in enumerate(stages):
        arrived = []
        for digit in order_of(stage):
            flip = (digit << shift) | 1
            arrived.append(lax.ppermute(block, "dev", [(d, d ^ flip) for d in range(count)]))
        if stage == 0:
            marked = mark(block)
            block, marked = lax.optimization_barrier((jnp.concatenate([block] + arrived, axis=0), marked))
            line = block
        else:
            block = jnp.concatenate([block] + arrived, axis=0)
    return line, block, marked


def mark_kernel(block_ref, out_ref):
    out_ref[...] = block_ref[0, 0:8, :].astype(jnp.float32)


def mark(block):
    vmem = pl.BlockSpec(memory_space=pltpu.VMEM)
    return pl.pallas_call(
        mark_kernel,
        out_shape=jax.ShapeDtypeStruct((8, block.shape[2]), jnp.float32),
        in_specs=[vmem],
        out_specs=vmem,
        compiler_params=pltpu.CompilerParams(vmem_limit_bytes=4 * 1024 * 1024),
        cost_estimate=pl.CostEstimate(flops=2**34, bytes_accessed=2**25, transcendentals=0),
    )(block)


def pack_kernel(q_hbm, c_hbm, out_ref, c_ref, sems):
    rows, lanes = q_hbm.shape
    cand = c_hbm.shape[1]
    q_copy = pltpu.make_async_copy(q_hbm, out_ref.at[0:rows], sems.at[0])
    c_copy = pltpu.make_async_copy(c_hbm, c_ref, sems.at[1])
    c_copy.start()
    q_copy.start()
    c_copy.wait()
    ids = c_ref[...]
    wide = jnp.concatenate([ids, jnp.zeros((2, lanes - cand), jnp.int32)], axis=1)
    lane = lax.broadcasted_iota(jnp.int32, (1, lanes), 1)
    flat = jnp.where(lane < cand, wide[0:1, :], pltpu.roll(wide, cand, 1)[1:2, :])
    row = lax.broadcasted_iota(jnp.int32, (ID_ROWS, lanes), 0)
    flat = jnp.broadcast_to(flat, (ID_ROWS, lanes))
    byte = jnp.where(row < 4, flat // 256, flat % 256)
    out_ref[rows:rows + ID_ROWS, :] = byte.astype(jnp.float32).astype(jnp.bfloat16)
    q_copy.wait()


def rows_of(blocks):
    return -(-blocks // 8) * 8


def ids_of(id_blocks):
    dim = id_blocks[0].shape[1]
    sublane = lax.broadcasted_iota(jnp.int32, (8, dim), 0)
    groups = []
    for first in range(0, len(id_blocks), 8):
        eight = jnp.full((8, dim), -1.0, jnp.float32)
        for four in range(first, min(first + 8, len(id_blocks)), 4):
            both = jnp.zeros((8, dim), jnp.float32)
            for s in range(four, four + 4):
                both = jnp.where(sublane % 4 == s - four, id_blocks[s].astype(jnp.float32), both)
            both = jnp.where(sublane < 4, both * 256.0, both)
            both = both + pltpu.roll(both, 4, 0)
            eight = jnp.where(sublane // 4 == (four - first) // 4, both, eight)
        groups.append(eight)
    return jnp.concatenate(groups, axis=0).astype(jnp.int32)


def score_kernel(cap, places, flips, n_earlier, len_hbm, p_ref, mark_ref, g_ref, *refs):
    p_local, ptok, dim = p_ref.shape
    last = n_earlier > 0
    earlier, refs = refs[:2 * n_earlier], refs[2 * n_earlier:]
    if last:
        out_ref, best, len_ref, len_sem = refs
    else:
        best, rank_ref, len_ref, len_sem = refs
    tokens = g_ref.shape[1] - ID_ROWS
    half = tokens // 2
    pairs = cap // 2
    rows = rows_of(len(places))
    me = lax.axis_index("dev")
    len_copy = pltpu.make_async_copy(len_hbm, len_ref, len_sem)
    len_copy.start()

    ids = ids_of([g_ref[place, tokens:tokens + ID_ROWS, :] for place in places])
    local = ids - me * p_local
    mine = (ids >= 0) & (local >= 0) & (local < p_local)
    before = lax.broadcasted_iota(jnp.int32, (dim, dim), 0) < lax.broadcasted_iota(jnp.int32, (dim, dim), 1)
    rank = jnp.dot(
        jnp.where(mine, 1.0, 0.0).astype(jnp.bfloat16),
        jnp.where(before, 1.0, 0.0).astype(jnp.bfloat16),
        preferred_element_type=jnp.float32,
    ).astype(jnp.int32)
    rank = jnp.where(mine, rank, -1)
    high, low = local // 256, local % 256
    entries = jnp.concatenate(
        [
            jnp.concatenate([jnp.where(rank == k, part, 0).astype(jnp.float32) for part in (high, low)], axis=1)
            for k in range(cap)
        ],
        axis=0,
    ).astype(jnp.bfloat16)
    weigh = jnp.where(lax.broadcasted_iota(jnp.int32, (8, 2 * dim), 1) < dim, 256.0, 1.0).astype(jnp.bfloat16)
    table = lax.dot_general(weigh, entries, NT, preferred_element_type=jnp.float32).astype(jnp.int32)
    len_copy.wait()

    left = lax.broadcasted_iota(jnp.int32, (8, dim), 1) < tokens
    token = lax.broadcasted_iota(jnp.int32, (8, dim), 0)
    if rows > len(places):
        best[...] = jnp.zeros_like(best)
    for i, place in enumerate(places):
        q = g_ref[place, 0:tokens, :]
        zero = jnp.zeros_like(q)
        weight = jnp.concatenate(
            [jnp.concatenate([q, zero], axis=1), jnp.concatenate([zero, q], axis=1)], axis=0
        )
        at = [table[0, k * rows + i] for k in range(cap)]
        x = jnp.concatenate(
            [jnp.concatenate([p_ref[at[p]], p_ref[at[p + pairs]]], axis=1) for p in range(pairs)], axis=0
        )
        sim = lax.dot_general(x, weight, NT, preferred_element_type=jnp.float32)
        for p in range(pairs):
            live = jnp.where(left, len_ref[at[p]], len_ref[at[p + pairs]])
            top = None
            for t in range(0, ptok, 8):
                part = sim[p * ptok + t:p * ptok + t + 8, :]
                if t + 8 > SHORTEST:
                    part = jnp.where(token + t < live, part, -1e30)
                top = part if top is None else jnp.maximum(top, part)
            best[p * rows + i:p * rows + i + 1, :] = jnp.max(top, axis=0, keepdims=True)

    if not last:
        rank_ref[...] = rank
        return

    lane_l = lax.broadcasted_iota(jnp.int32, (3 * dim, 2 * dim), 0) % dim
    lane_j = lax.broadcasted_iota(jnp.int32, (3 * dim, 2 * dim), 1)
    spread = (lane_l // half == lane_j // (dim // 2))
    spread = jnp.where(spread, 1.0, 0.0).astype(jnp.bfloat16)

    at = 0
    for best, rank in [(earlier[2 * c][...], earlier[2 * c + 1][...]) for c in range(n_earlier)] + [(best[...], rank)]:
        rows = rank.shape[0]
        hi = best.astype(jnp.bfloat16)
        rest = best - hi.astype(jnp.float32)
        mid = rest.astype(jnp.bfloat16)
        low = (rest - mid.astype(jnp.float32)).astype(jnp.bfloat16)
        sums = jnp.dot(jnp.concatenate([hi, mid, low], axis=1), spread, preferred_element_type=jnp.float32)
        total = jnp.zeros((rows, dim), jnp.float32)
        for p in range(pairs):
            part = sums[p * rows:(p + 1) * rows, :]
            total = jnp.where(rank == p, part[:, 0:dim], total)
            total = jnp.where(rank == p + pairs, part[:, dim:2 * dim], total)
        rolled = pltpu.roll(total, dim // 2, 1)
        for i, flip in enumerate(flips[at]):
            device = me ^ flip
            out_ref[pl.ds(device, 1), 0, :] = total[i:i + 1, :]
            out_ref[pl.ds(device, 1), 1, :] = rolled[i:i + 1, :]
        at += 1


def score(count, cap, places, flips, lengths, passages, marked, blocks, earlier=()):
    dim = passages.shape[2]
    anywhere, vmem = pl.BlockSpec(memory_space=pl.ANY), pl.BlockSpec(memory_space=pltpu.VMEM)
    rows = rows_of(len(places))
    best = ((cap // 2) * rows, dim)
    scratch = [pltpu.SMEM(lengths.shape, jnp.int32), pltpu.SemaphoreType.DMA]
    if earlier:
        scratch = [pltpu.VMEM(best, jnp.float32)] + scratch
        shapes, out_specs = jax.ShapeDtypeStruct((count, 2, dim), jnp.float32), vmem
    else:
        shapes = [jax.ShapeDtypeStruct(best, jnp.float32), jax.ShapeDtypeStruct((rows, dim), jnp.int32)]
        out_specs = [vmem, vmem]
    return pl.pallas_call(
        functools.partial(score_kernel, cap, places, flips, len(earlier) // 2),
        out_shape=shapes,
        in_specs=[anywhere, vmem, anywhere] + [vmem] * (1 + len(earlier)),
        out_specs=out_specs,
        scratch_shapes=scratch,
        compiler_params=pltpu.CompilerParams(vmem_limit_bytes=24 * 1024 * 1024),
    )(lengths, passages, marked, blocks, *earlier)


def on_device(queries, passages, lengths, candidates):
    count = lax.axis_size("dev")
    q_local, qtok, dim = queries.shape
    cand = candidates.shape[1]
    slots = q_local * cand
    cap = 2 * ((slots + count - 1) // count)
    rows = q_local * qtok

    packed = pl.pallas_call(
        pack_kernel,
        out_shape=jax.ShapeDtypeStruct((rows + ID_ROWS, dim), jnp.bfloat16),
        in_specs=[pl.BlockSpec(memory_space=pl.ANY), pl.BlockSpec(memory_space=pl.ANY)],
        out_specs=pl.BlockSpec(memory_space=pltpu.VMEM),
        scratch_shapes=[pltpu.VMEM(candidates.shape, jnp.int32), pltpu.SemaphoreType.DMA((2,))],
        compiler_params=pltpu.CompilerParams(vmem_limit_bytes=4 * 1024 * 1024),
    )(
        pltpu.with_memory_space_constraint(queries.reshape(rows, dim), pltpu.HBM),
        pltpu.with_memory_space_constraint(candidates, pltpu.HBM),
    )
    stages = stages_of(count)[:-1]
    sibling = [(d, d ^ 1) for d in range(count)]
    line, blocks, marked = gather_blocks(packed[None], stages, count)
    flips = flips_of(stages)
    first, every = line.shape[0], len(flips)
    line_call = score(count, cap, range(first), (), lengths, passages, marked, line)
    blocks, *line_call = lax.optimization_barrier((blocks, *line_call))
    others = lax.ppermute(blocks, "dev", sibling)
    rest_call = score(count, cap, range(first, every), (), lengths, passages, marked, blocks)
    devices = (flips[:first], flips[first:], [flip ^ 1 for flip in flips])
    dense = score(
        count, cap, range(every), devices, lengths, passages, marked, others, (*line_call, *rest_call)
    )
    back = lax.all_to_all(dense, "dev", split_axis=0, concat_axis=0, tiled=True)
    return jnp.sum(back, axis=0)[:, 0:cand]


def solution(mesh):
    return jax.shard_map(
        on_device,
        mesh=mesh,
        in_specs=(P("dev", None, None), P("dev", None, None), P("dev"), P("dev", None)),
        out_specs=P("dev", None),
        check_vma=False,
    )
```

```python
import functools

import jax
import jax.numpy as jnp
from jax import lax
from jax.experimental import pallas as pl
from jax.experimental.pallas import tpu as pltpu
from jax.sharding import PartitionSpec as P

MESH_BITS = 2
SHORTEST = 16
NT = (((1,), (1,)), ((), ()))
ID_ROWS = 8


def stages_of(count):
    stages, high = [], count.bit_length() - 1
    while high > 0:
        width = min(MESH_BITS, high)
        stages.append((high - width, 1 << width))
        high -= width
    return stages


def order_of(stage):
    return (1, 3, 2) if stage == 0 else (3, 2, 1)


def flips_of(stages):
    flips = [0]
    for stage, (shift, size) in enumerate(stages):
        flips = [flip ^ ((digit << shift) | 1 if digit else 0) for digit in (0,) + order_of(stage) for flip in flips]
    return flips


def gather_blocks(block, stages, count):
    def send(block, shift, digit):
        flip = (digit << shift) | 1
        return lax.ppermute(block, "dev", [(d, d ^ flip) for d in range(count)])

    (near, _), (far, _) = stages[:2]
    arrived = [send(block, near, digit) for digit in order_of(0)]
    marked = mark(block, 2**20)
    own, marked = lax.optimization_barrier((block, marked))
    *soon, last = order_of(1)
    early = [send(own, far, digit) for digit in soon]
    others = jnp.concatenate(arrived, axis=0)
    line = jnp.concatenate([block, others], axis=0)
    line, others, marked = lax.optimization_barrier((line, others, mark(line, 2**34) + marked))
    late = [send(others, far, digit) for digit in soon]
    parts = [part for pair in zip(early, late) for part in pair] + [send(line, far, last)]
    block = jnp.concatenate([line] + parts, axis=0)
    for stage, (shift, size) in enumerate(stages[2:], 2):
        block = jnp.concatenate([block] + [send(block, shift, digit) for digit in order_of(stage)], axis=0)
    return line, block, marked


def mark_kernel(block_ref, out_ref):
    out_ref[...] = block_ref[0, 0:8, :].astype(jnp.float32)


def mark(block, flops):
    vmem = pl.BlockSpec(memory_space=pltpu.VMEM)
    return pl.pallas_call(
        mark_kernel,
        out_shape=jax.ShapeDtypeStruct((8, block.shape[2]), jnp.float32),
        in_specs=[vmem],
        out_specs=vmem,
        compiler_params=pltpu.CompilerParams(vmem_limit_bytes=4 * 1024 * 1024),
        cost_estimate=pl.CostEstimate(flops=flops, bytes_accessed=flops >> 9, transcendentals=0),
    )(block)


def pack_kernel(q_hbm, c_hbm, out_ref, c_ref, sems):
    rows, lanes = q_hbm.shape
    cand = c_hbm.shape[1]
    q_copy = pltpu.make_async_copy(q_hbm, out_ref.at[0:rows], sems.at[0])
    c_copy = pltpu.make_async_copy(c_hbm, c_ref, sems.at[1])
    c_copy.start()
    q_copy.start()
    c_copy.wait()
    ids = c_ref[...]
    wide = jnp.concatenate([ids, jnp.zeros((2, lanes - cand), jnp.int32)], axis=1)
    lane = lax.broadcasted_iota(jnp.int32, (1, lanes), 1)
    flat = jnp.where(lane < cand, wide[0:1, :], pltpu.roll(wide, cand, 1)[1:2, :])
    row = lax.broadcasted_iota(jnp.int32, (ID_ROWS, lanes), 0)
    flat = jnp.broadcast_to(flat, (ID_ROWS, lanes))
    byte = jnp.where(row < 4, flat // 256, flat % 256)
    out_ref[rows:rows + ID_ROWS, :] = byte.astype(jnp.float32).astype(jnp.bfloat16)
    q_copy.wait()


def rows_of(blocks):
    return -(-blocks // 8) * 8


def ids_of(id_blocks):
    dim = id_blocks[0].shape[1]
    sublane = lax.broadcasted_iota(jnp.int32, (8, dim), 0)
    groups = []
    for first in range(0, len(id_blocks), 8):
        eight = jnp.full((8, dim), -1.0, jnp.float32)
        for four in range(first, min(first + 8, len(id_blocks)), 4):
            both = jnp.zeros((8, dim), jnp.float32)
            for s in range(four, four + 4):
                both = jnp.where(sublane % 4 == s - four, id_blocks[s].astype(jnp.float32), both)
            both = jnp.where(sublane < 4, both * 256.0, both)
            both = both + pltpu.roll(both, 4, 0)
            eight = jnp.where(sublane // 4 == (four - first) // 4, both, eight)
        groups.append(eight)
    return jnp.concatenate(groups, axis=0).astype(jnp.int32)


def score_kernel(cap, places, flips, n_earlier, len_hbm, p_ref, mark_ref, g_ref, *refs):
    p_local, ptok, dim = p_ref.shape
    last = n_earlier > 0
    earlier, refs = refs[:2 * n_earlier], refs[2 * n_earlier:]
    if last:
        out_ref, best, len_ref, len_sem = refs
    else:
        best, rank_ref, len_ref, len_sem = refs
    tokens = g_ref.shape[1] - ID_ROWS
    half = tokens // 2
    pairs = cap // 2
    rows = rows_of(len(places))
    me = lax.axis_index("dev")
    len_copy = pltpu.make_async_copy(len_hbm, len_ref, len_sem)
    len_copy.start()

    ids = ids_of([g_ref[place, tokens:tokens + ID_ROWS, :] for place in places])
    local = ids - me * p_local
    mine = (ids >= 0) & (local >= 0) & (local < p_local)
    before = lax.broadcasted_iota(jnp.int32, (dim, dim), 0) < lax.broadcasted_iota(jnp.int32, (dim, dim), 1)
    rank = jnp.dot(
        jnp.where(mine, 1.0, 0.0).astype(jnp.bfloat16),
        jnp.where(before, 1.0, 0.0).astype(jnp.bfloat16),
        preferred_element_type=jnp.float32,
    ).astype(jnp.int32)
    rank = jnp.where(mine, rank, -1)
    high, low = local // 256, local % 256
    entries = jnp.concatenate(
        [
            jnp.concatenate([jnp.where(rank == k, part, 0).astype(jnp.float32) for part in (high, low)], axis=1)
            for k in range(cap)
        ],
        axis=0,
    ).astype(jnp.bfloat16)
    weigh = jnp.where(lax.broadcasted_iota(jnp.int32, (8, 2 * dim), 1) < dim, 256.0, 1.0).astype(jnp.bfloat16)
    table = lax.dot_general(weigh, entries, NT, preferred_element_type=jnp.float32).astype(jnp.int32)
    len_copy.wait()

    left = lax.broadcasted_iota(jnp.int32, (8, dim), 1) < tokens
    token = lax.broadcasted_iota(jnp.int32, (8, dim), 0)
    if rows > len(places):
        best[...] = jnp.zeros_like(best)
    for i, place in enumerate(places):
        q = g_ref[place, 0:tokens, :]
        zero = jnp.zeros_like(q)
        weight = jnp.concatenate(
            [jnp.concatenate([q, zero], axis=1), jnp.concatenate([zero, q], axis=1)], axis=0
        )
        at = [table[0, k * rows + i] for k in range(cap)]
        x = jnp.concatenate(
            [jnp.concatenate([p_ref[at[p]], p_ref[at[p + pairs]]], axis=1) for p in range(pairs)], axis=0
        )
        sim = lax.dot_general(x, weight, NT, preferred_element_type=jnp.float32)
        for p in range(pairs):
            live = jnp.where(left, len_ref[at[p]], len_ref[at[p + pairs]])
            top = None
            for t in range(0, ptok, 8):
                part = sim[p * ptok + t:p * ptok + t + 8, :]
                if t + 8 > SHORTEST:
                    part = jnp.where(token + t < live, part, -1e30)
                top = part if top is None else jnp.maximum(top, part)
            best[p * rows + i:p * rows + i + 1, :] = jnp.max(top, axis=0, keepdims=True)

    if not last:
        rank_ref[...] = rank
        return

    lane_l = lax.broadcasted_iota(jnp.int32, (3 * dim, 2 * dim), 0) % dim
    lane_j = lax.broadcasted_iota(jnp.int32, (3 * dim, 2 * dim), 1)
    spread = (lane_l // half == lane_j // (dim // 2))
    spread = jnp.where(spread, 1.0, 0.0).astype(jnp.bfloat16)

    at = 0
    for best, rank in [(earlier[2 * c][...], earlier[2 * c + 1][...]) for c in range(n_earlier)] + [(best[...], rank)]:
        rows = rank.shape[0]
        hi = best.astype(jnp.bfloat16)
        rest = best - hi.astype(jnp.float32)
        mid = rest.astype(jnp.bfloat16)
        low = (rest - mid.astype(jnp.float32)).astype(jnp.bfloat16)
        sums = jnp.dot(jnp.concatenate([hi, mid, low], axis=1), spread, preferred_element_type=jnp.float32)
        total = jnp.zeros((rows, dim), jnp.float32)
        for p in range(pairs):
            part = sums[p * rows:(p + 1) * rows, :]
            total = jnp.where(rank == p, part[:, 0:dim], total)
            total = jnp.where(rank == p + pairs, part[:, dim:2 * dim], total)
        for i, flip in enumerate(flips[at]):
            out_ref[pl.ds(me ^ flip, 1), :] = total[i:i + 1, :]
        at += 1


def score(count, cap, places, flips, lengths, passages, marked, blocks, earlier=()):
    dim = passages.shape[2]
    anywhere, vmem = pl.BlockSpec(memory_space=pl.ANY), pl.BlockSpec(memory_space=pltpu.VMEM)
    rows = rows_of(len(places))
    best = ((cap // 2) * rows, dim)
    scratch = [pltpu.SMEM(lengths.shape, jnp.int32), pltpu.SemaphoreType.DMA]
    if earlier:
        scratch = [pltpu.VMEM(best, jnp.float32)] + scratch
        shapes, out_specs = jax.ShapeDtypeStruct((count, dim), jnp.float32), vmem
    else:
        shapes = [jax.ShapeDtypeStruct(best, jnp.float32), jax.ShapeDtypeStruct((rows, dim), jnp.int32)]
        out_specs = [vmem, vmem]
    return pl.pallas_call(
        functools.partial(score_kernel, cap, places, flips, len(earlier) // 2),
        out_shape=shapes,
        in_specs=[anywhere, vmem, anywhere] + [vmem] * (1 + len(earlier)),
        out_specs=out_specs,
        scratch_shapes=scratch,
        compiler_params=pltpu.CompilerParams(vmem_limit_bytes=24 * 1024 * 1024),
    )(lengths, passages, marked, blocks, *earlier)


def sum_kernel(rows_ref, out_ref):
    cand = out_ref.shape[1]
    total = jnp.sum(rows_ref[...], axis=0, keepdims=True)
    total = jnp.broadcast_to(total, (8, 2 * cand))
    out_ref[0:1, :] = total[0:1, 0:cand]
    out_ref[1:2, :] = pltpu.roll(total, cand, 1)[0:1, 0:cand]


def on_device(queries, passages, lengths, candidates):
    count = lax.axis_size("dev")
    q_local, qtok, dim = queries.shape
    cand = candidates.shape[1]
    slots = q_local * cand
    cap = 2 * ((slots + count - 1) // count)
    rows = q_local * qtok

    packed = pl.pallas_call(
        pack_kernel,
        out_shape=jax.ShapeDtypeStruct((rows + ID_ROWS, dim), jnp.bfloat16),
        in_specs=[pl.BlockSpec(memory_space=pl.ANY), pl.BlockSpec(memory_space=pl.ANY)],
        out_specs=pl.BlockSpec(memory_space=pltpu.VMEM),
        scratch_shapes=[pltpu.VMEM(candidates.shape, jnp.int32), pltpu.SemaphoreType.DMA((2,))],
        compiler_params=pltpu.CompilerParams(vmem_limit_bytes=4 * 1024 * 1024),
    )(
        pltpu.with_memory_space_constraint(queries.reshape(rows, dim), pltpu.HBM),
        pltpu.with_memory_space_constraint(candidates, pltpu.HBM),
    )
    stages = stages_of(count)[:-1]
    sibling = [(d, d ^ 1) for d in range(count)]
    line, blocks, marked = gather_blocks(packed[None], stages, count)
    flips = flips_of(stages)
    first, every = line.shape[0], len(flips)
    line_call = score(count, cap, range(first), (), lengths, passages, marked, line)
    blocks, *line_call = lax.optimization_barrier((blocks, *line_call))
    others = lax.ppermute(blocks, "dev", sibling)
    rest_call = score(count, cap, range(first, every), (), lengths, passages, marked, blocks)
    devices = (flips[:first], flips[first:], [flip ^ 1 for flip in flips])
    dense = score(
        count, cap, range(every), devices, lengths, passages, marked, others, (*line_call, *rest_call)
    )
    back = lax.all_to_all(dense, "dev", split_axis=0, concat_axis=0, tiled=True)
    vmem = pl.BlockSpec(memory_space=pltpu.VMEM)
    return pl.pallas_call(
        sum_kernel,
        out_shape=jax.ShapeDtypeStruct((q_local, cand), jnp.float32),
        in_specs=[vmem],
        out_specs=vmem,
        compiler_params=pltpu.CompilerParams(vmem_limit_bytes=4 * 1024 * 1024),
    )(back)


def solution(mesh):
    return jax.shard_map(
        on_device,
        mesh=mesh,
        in_specs=(P("dev", None, None), P("dev", None, None), P("dev"), P("dev", None)),
        out_specs=P("dev", None),
        check_vma=False,
    )
```

```python
import functools

import jax
import jax.numpy as jnp
from jax import lax
from jax.experimental import pallas as pl
from jax.experimental.pallas import tpu as pltpu
from jax.sharding import PartitionSpec as P

MESH_BITS = 2
SHORTEST = 16
NT = (((1,), (1,)), ((), ()))
ID_ROWS = 8


def stages_of(count):
    stages, high = [], count.bit_length() - 1
    while high > 0:
        width = min(MESH_BITS, high)
        stages.append((high - width, 1 << width))
        high -= width
    return stages


def order_of(stage):
    return (2, 3, 1) if stage == 0 else (3, 2, 1)


def flips_of(stages):
    flips = [0]
    for stage, (shift, size) in enumerate(stages):
        flips = [flip ^ ((digit << shift) | 1 if digit else 0) for digit in (0,) + order_of(stage) for flip in flips]
    return flips


def gather_blocks(block, stages, count):
    def send(block, shift, digit):
        flip = (digit << shift) | 1
        return lax.ppermute(block, "dev", [(d, d ^ flip) for d in range(count)])

    (near, _), (far, _) = stages[:2]
    arrived = [send(block, near, digit) for digit in order_of(0)]
    marked = mark(block, 2**20)
    own, marked = lax.optimization_barrier((block, marked))
    *soon, last = order_of(1)
    early = [send(own, far, digit) for digit in soon]
    others = jnp.concatenate(arrived, axis=0)
    line = jnp.concatenate([block, others], axis=0)
    line, others, marked = lax.optimization_barrier((line, others, mark(line, 2**34) + marked))
    late = [send(others, far, digit) for digit in soon]
    parts = [part for pair in zip(early, late) for part in pair] + [send(line, far, last)]
    rest = jnp.concatenate(parts, axis=0)
    for stage, (shift, size) in enumerate(stages[2:], 2):
        block = jnp.concatenate([line, rest], axis=0)
        rest = jnp.concatenate([rest] + [send(block, shift, digit) for digit in order_of(stage)], axis=0)
    return line, rest, marked


def mark_kernel(block_ref, out_ref):
    out_ref[...] = block_ref[0, 0:8, :].astype(jnp.float32)


def mark(block, flops):
    vmem = pl.BlockSpec(memory_space=pltpu.VMEM)
    return pl.pallas_call(
        mark_kernel,
        out_shape=jax.ShapeDtypeStruct((8, block.shape[2]), jnp.float32),
        in_specs=[vmem],
        out_specs=vmem,
        compiler_params=pltpu.CompilerParams(vmem_limit_bytes=4 * 1024 * 1024),
        cost_estimate=pl.CostEstimate(flops=flops, bytes_accessed=flops >> 9, transcendentals=0),
    )(block)


def pack_kernel(q_hbm, c_hbm, out_ref, c_ref, sems):
    rows, lanes = q_hbm.shape
    cand = c_hbm.shape[1]
    q_copy = pltpu.make_async_copy(q_hbm, out_ref.at[0:rows], sems.at[0])
    c_copy = pltpu.make_async_copy(c_hbm, c_ref, sems.at[1])
    c_copy.start()
    q_copy.start()
    c_copy.wait()
    ids = c_ref[...]
    wide = jnp.concatenate([ids, jnp.zeros((2, lanes - cand), jnp.int32)], axis=1)
    lane = lax.broadcasted_iota(jnp.int32, (1, lanes), 1)
    flat = jnp.where(lane < cand, wide[0:1, :], pltpu.roll(wide, cand, 1)[1:2, :])
    row = lax.broadcasted_iota(jnp.int32, (ID_ROWS, lanes), 0)
    flat = jnp.broadcast_to(flat, (ID_ROWS, lanes))
    byte = jnp.where(row < 4, flat // 256, flat % 256)
    out_ref[rows:rows + ID_ROWS, :] = byte.astype(jnp.float32).astype(jnp.bfloat16)
    q_copy.wait()


def rows_of(blocks):
    return -(-blocks // 8) * 8


def ids_of(id_blocks):
    dim = id_blocks[0].shape[1]
    sublane = lax.broadcasted_iota(jnp.int32, (8, dim), 0)
    groups = []
    for first in range(0, len(id_blocks), 8):
        eight = jnp.full((8, dim), -1.0, jnp.float32)
        for four in range(first, min(first + 8, len(id_blocks)), 4):
            both = jnp.zeros((8, dim), jnp.float32)
            for s in range(four, four + 4):
                both = jnp.where(sublane % 4 == s - four, id_blocks[s].astype(jnp.float32), both)
            both = jnp.where(sublane < 4, both * 256.0, both)
            both = both + pltpu.roll(both, 4, 0)
            eight = jnp.where(sublane // 4 == (four - first) // 4, both, eight)
        groups.append(eight)
    return jnp.concatenate(groups, axis=0).astype(jnp.int32)


def score_kernel(cap, n_sets, flips, n_earlier, len_hbm, p_ref, mark_ref, *refs):
    p_local, ptok, dim = p_ref.shape
    last = n_earlier > 0
    sets, refs = refs[:n_sets], refs[n_sets:]
    places = [(g_ref, place) for g_ref in sets for place in range(g_ref.shape[0])]
    earlier, refs = refs[:2 * n_earlier], refs[2 * n_earlier:]
    if last:
        out_ref, best, len_ref, len_sem = refs
    else:
        best, rank_ref, len_ref, len_sem = refs
    tokens = sets[0].shape[1] - ID_ROWS
    half = tokens // 2
    pairs = cap // 2
    rows = rows_of(len(places))
    me = lax.axis_index("dev")
    len_copy = pltpu.make_async_copy(len_hbm, len_ref, len_sem)
    len_copy.start()

    ids = ids_of([g_ref[place, tokens:tokens + ID_ROWS, :] for g_ref, place in places])
    local = ids - me * p_local
    mine = (ids >= 0) & (local >= 0) & (local < p_local)
    before = lax.broadcasted_iota(jnp.int32, (dim, dim), 0) < lax.broadcasted_iota(jnp.int32, (dim, dim), 1)
    rank = jnp.dot(
        jnp.where(mine, 1.0, 0.0).astype(jnp.bfloat16),
        jnp.where(before, 1.0, 0.0).astype(jnp.bfloat16),
        preferred_element_type=jnp.float32,
    ).astype(jnp.int32)
    rank = jnp.where(mine, rank, -1)
    high, low = local // 256, local % 256
    entries = jnp.concatenate(
        [
            jnp.concatenate([jnp.where(rank == k, part, 0).astype(jnp.float32) for part in (high, low)], axis=1)
            for k in range(cap)
        ],
        axis=0,
    ).astype(jnp.bfloat16)
    weigh = jnp.where(lax.broadcasted_iota(jnp.int32, (8, 2 * dim), 1) < dim, 256.0, 1.0).astype(jnp.bfloat16)
    table = lax.dot_general(weigh, entries, NT, preferred_element_type=jnp.float32).astype(jnp.int32)
    len_copy.wait()

    left = lax.broadcasted_iota(jnp.int32, (8, dim), 1) < tokens
    token = lax.broadcasted_iota(jnp.int32, (8, dim), 0)
    if rows > len(places):
        best[...] = jnp.zeros_like(best)
    for i, (g_ref, place) in enumerate(places):
        q = g_ref[place, 0:tokens, :]
        zero = jnp.zeros_like(q)
        weight = jnp.concatenate(
            [jnp.concatenate([q, zero], axis=1), jnp.concatenate([zero, q], axis=1)], axis=0
        )
        at = [table[0, k * rows + i] for k in range(cap)]
        x = jnp.concatenate(
            [jnp.concatenate([p_ref[at[p]], p_ref[at[p + pairs]]], axis=1) for p in range(pairs)], axis=0
        )
        sim = lax.dot_general(x, weight, NT, preferred_element_type=jnp.float32)
        for p in range(pairs):
            live = jnp.where(left, len_ref[at[p]], len_ref[at[p + pairs]])
            top = None
            for t in range(0, ptok, 8):
                part = sim[p * ptok + t:p * ptok + t + 8, :]
                if t + 8 > SHORTEST:
                    part = jnp.where(token + t < live, part, -1e30)
                top = part if top is None else jnp.maximum(top, part)
            best[p * rows + i:p * rows + i + 1, :] = jnp.max(top, axis=0, keepdims=True)

    if not last:
        rank_ref[...] = rank
        return

    lane_l = lax.broadcasted_iota(jnp.int32, (3 * dim, 2 * dim), 0) % dim
    lane_j = lax.broadcasted_iota(jnp.int32, (3 * dim, 2 * dim), 1)
    spread = (lane_l // half == lane_j // (dim // 2))
    spread = jnp.where(spread, 1.0, 0.0).astype(jnp.bfloat16)

    at = 0
    for best, rank in [(earlier[2 * c][...], earlier[2 * c + 1][...]) for c in range(n_earlier)] + [(best[...], rank)]:
        rows = rank.shape[0]
        hi = best.astype(jnp.bfloat16)
        rest = best - hi.astype(jnp.float32)
        mid = rest.astype(jnp.bfloat16)
        low = (rest - mid.astype(jnp.float32)).astype(jnp.bfloat16)
        sums = jnp.dot(jnp.concatenate([hi, mid, low], axis=1), spread, preferred_element_type=jnp.float32)
        total = jnp.zeros((rows, dim), jnp.float32)
        for p in range(pairs):
            part = sums[p * rows:(p + 1) * rows, :]
            total = jnp.where(rank == p, part[:, 0:dim], total)
            total = jnp.where(rank == p + pairs, part[:, dim:2 * dim], total)
        for i, flip in enumerate(flips[at]):
            out_ref[pl.ds(me ^ flip, 1), :] = total[i:i + 1, :]
        at += 1


def score(count, cap, flips, lengths, passages, marked, sets, earlier=()):
    dim = passages.shape[2]
    anywhere, vmem = pl.BlockSpec(memory_space=pl.ANY), pl.BlockSpec(memory_space=pltpu.VMEM)
    rows = rows_of(sum(blocks.shape[0] for blocks in sets))
    best = ((cap // 2) * rows, dim)
    scratch = [pltpu.SMEM(lengths.shape, jnp.int32), pltpu.SemaphoreType.DMA]
    if earlier:
        scratch = [pltpu.VMEM(best, jnp.float32)] + scratch
        shapes, out_specs = jax.ShapeDtypeStruct((count, dim), jnp.float32), vmem
    else:
        shapes = [jax.ShapeDtypeStruct(best, jnp.float32), jax.ShapeDtypeStruct((rows, dim), jnp.int32)]
        out_specs = [vmem, vmem]
    return pl.pallas_call(
        functools.partial(score_kernel, cap, len(sets), flips, len(earlier) // 2),
        out_shape=shapes,
        in_specs=[anywhere, vmem, anywhere] + [vmem] * (len(sets) + len(earlier)),
        out_specs=out_specs,
        scratch_shapes=scratch,
        compiler_params=pltpu.CompilerParams(vmem_limit_bytes=24 * 1024 * 1024),
    )(lengths, passages, marked, *sets, *earlier)


def sum_kernel(rows_ref, out_ref):
    cand = out_ref.shape[1]
    total = jnp.sum(rows_ref[...], axis=0, keepdims=True)
    total = jnp.broadcast_to(total, (8, 2 * cand))
    out_ref[0:1, :] = total[0:1, 0:cand]
    out_ref[1:2, :] = pltpu.roll(total, cand, 1)[0:1, 0:cand]


def on_device(queries, passages, lengths, candidates):
    count = lax.axis_size("dev")
    q_local, qtok, dim = queries.shape
    cand = candidates.shape[1]
    slots = q_local * cand
    cap = 2 * ((slots + count - 1) // count)
    rows = q_local * qtok

    packed = pl.pallas_call(
        pack_kernel,
        out_shape=jax.ShapeDtypeStruct((rows + ID_ROWS, dim), jnp.bfloat16),
        in_specs=[pl.BlockSpec(memory_space=pl.ANY), pl.BlockSpec(memory_space=pl.ANY)],
        out_specs=pl.BlockSpec(memory_space=pltpu.VMEM),
        scratch_shapes=[pltpu.VMEM(candidates.shape, jnp.int32), pltpu.SemaphoreType.DMA((2,))],
        compiler_params=pltpu.CompilerParams(vmem_limit_bytes=4 * 1024 * 1024),
    )(
        pltpu.with_memory_space_constraint(queries.reshape(rows, dim), pltpu.HBM),
        pltpu.with_memory_space_constraint(candidates, pltpu.HBM),
    )
    stages = stages_of(count)[:-1]
    sibling = [(d, d ^ 1) for d in range(count)]
    line, rest, marked = gather_blocks(packed[None], stages, count)
    flips = flips_of(stages)
    first = line.shape[0]
    line_call = score(count, cap, (), lengths, passages, marked, (line,))
    other_line = lax.ppermute(line, "dev", sibling)
    rest, other_line, *line_call = lax.optimization_barrier((rest, other_line, *line_call))
    others = lax.ppermute(rest, "dev", sibling)
    rest_call = score(count, cap, (), lengths, passages, marked, (rest,))
    devices = (flips[:first], flips[first:], [flip ^ 1 for flip in flips])
    dense = score(
        count, cap, devices, lengths, passages, marked, (other_line, others), (*line_call, *rest_call)
    )
    back = lax.all_to_all(dense, "dev", split_axis=0, concat_axis=0, tiled=True)
    vmem = pl.BlockSpec(memory_space=pltpu.VMEM)
    return pl.pallas_call(
        sum_kernel,
        out_shape=jax.ShapeDtypeStruct((q_local, cand), jnp.float32),
        in_specs=[vmem],
        out_specs=vmem,
        compiler_params=pltpu.CompilerParams(vmem_limit_bytes=4 * 1024 * 1024),
    )(back)


def solution(mesh):
    return jax.shard_map(
        on_device,
        mesh=mesh,
        in_specs=(P("dev", None, None), P("dev", None, None), P("dev"), P("dev", None)),
        out_specs=P("dev", None),
        check_vma=False,
    )
```
